1024 devices in a mesh: path: 64 (over z, x), fsdp: 16 (over y, core).
Axes of the slice: x: 8, y: 8, z: 8, core: 2. Of those that a mesh axis runs over, the one named last changes fastest.
Arguments:
- token_pool: bfloat16 [512, 2048], P(None, 'fsdp'), may hold values from -6 to 6
- batch_ids: int32 [64, 1024], P('path'), may hold values from 0 to 511
- module_table: int32 [64], replicated, may hold values from 0 to 15, as said below
- cotangent: bfloat16 [64, 1024, 2048], P('path', None, 'fsdp'), may hold values from -6 to 6
- path_weights: bfloat16 [64, 2048, 2048], P('path', None, 'fsdp'), may hold values from -5 to 5
- first_moment: bfloat16 [64, 2048, 2048], P('path', None, 'fsdp'), may hold values from -2 to 2
- second_moment: bfloat16 [64, 2048, 2048], P('path', None, 'fsdp'), may hold values from 0.0099487305 to 1
- master_weights: float32 [16, 2048, 2048], P(None, 'path', 'fsdp'), may hold values from -5 to 5
- outer_momentum: float32 [16, 2048, 2048], P(None, 'path', 'fsdp'), may hold values from -3 to 3
Outputs:
- new_master: float32 [16, 2048, 2048], P(None, 'path', 'fsdp')
- new_momentum: float32 [16, 2048, 2048], P(None, 'path', 'fsdp')
- first_average: bfloat16 [16, 2048, 2048], P(None, 'path', 'fsdp')
- second_average: bfloat16 [16, 2048, 2048], P(None, 'path', 'fsdp')
The draws below stay inside these ranges and needn't reach their ends.
Inputs may be any that keep to these rules, and one draw needn't show every extreme that they name: `module_table`: the module each path visits; at least one of the 16 modules is visited by no path.
All inputs are finite; a program needn't handle non-finite values.
Results may differ from the reference program's by a relative error of at most 0.0033.
Values may be sent and summed in bfloat16 or wider, within the bound.
No kernel may reach another device: no remote copies, remote signals or barrier semaphores. Data moves between devices by JAX's collectives and lax.ppermute only.
A program may use at most 32 MiB of HBM per device.

```python
import math
import jax
import jax.numpy as jnp
from jax import lax

D = 2048
MODULES = 16
TOK = 1024
POOL = 512
PATHS = 64


def draw_module_table(key, part):
    key = jax.random.fold_in(key, 11)
    first_key, second_key, third_key, fourth_key, fifth_key = jax.random.split(key, 5)
    first_pick = jax.random.randint(first_key, (PATHS,), 0, MODULES - 3)
    second_pick = jax.random.randint(second_key, (PATHS,), 0, MODULES - 3)
    skewed = first_pick * second_pick // (MODULES - 4)
    relabel = (jax.random.permutation(third_key, MODULES - 2) + 1).astype(jnp.int32)
    table = jnp.take(relabel, skewed, axis=0).astype(jnp.int32)
    low_path = jax.random.randint(fourth_key, (), 0, PATHS)
    high_path = (low_path + 1 + jax.random.randint(fifth_key, (), 0, PATHS - 1)) % PATHS
    positions = jnp.arange(PATHS, dtype=jnp.int32)
    table = jnp.where(positions == low_path, 0, table)
    table = jnp.where(positions == high_path, MODULES - 1, table)
    return table.astype(jnp.int32)


def with_ends(array, own_key, low, high):
    dims = array.shape
    spot = [jax.random.randint(jax.random.fold_in(own_key, axis), (), 0, dims[axis]) for axis in range(len(dims))]
    array = array.at[tuple(spot)].set(low)
    longest = dims.index(max(dims))
    spot[longest] = (spot[longest] + 1) % dims[longest]
    return array.at[tuple(spot)].set(high)


def level_of(stream_key, dims, pieces, low, high):
    def one(axis_at, parts):
        steps = jax.random.uniform(jax.random.fold_in(jax.random.fold_in(stream_key, 6), axis_at), (parts,), jnp.float32, low / len(pieces), high / len(pieces))
        return jnp.repeat(jnp.exp(steps), dims[axis_at] // parts).reshape((-1,) + (1,) * (len(dims) - axis_at - 1))

    loudness = one(*pieces[0])
    for cut in pieces[1:]:
        loudness = loudness * one(*cut)
    return loudness


def noise(key, dims, spread, limit, cuts=(), held_as=jnp.bfloat16):
    gain = level_of(key, dims, cuts, -0.22, 0.18) if cuts else 1.0
    entries = jax.random.normal(key, dims, jnp.float32) * spread * gain
    return jnp.minimum(jnp.maximum(entries, -limit), limit).astype(held_as)


def setup_inputs(seed: int = 0) -> dict:
    splits = jax.random.split(jax.random.key(seed), 10)
    return {
        "token_pool": noise(splits[0], (POOL, D), 1.0, 6.0, ((1, 16),)),
        "batch_ids": with_ends(jax.random.randint(splits[1], (PATHS, TOK), 0, POOL), jax.random.fold_in(splits[1], 1), 0, POOL - 1).astype(jnp.int32),
        "module_table": draw_module_table(jax.random.fold_in(splits[9], 71), 0),
        "cotangent": noise(splits[3], (PATHS, TOK, D), 1.0, 6.0, ((0, 64), (2, 16))),
        "path_weights": noise(splits[4], (PATHS, D, D), 1.0, 5.0, ((0, 64), (2, 16))),
        "first_moment": noise(splits[5], (PATHS, D, D), 0.3, 2.0, ((0, 64), (2, 16))),
        "second_moment": jnp.clip(jnp.exp(math.log(1.0) - 4.61031033 * jax.random.uniform(splits[6], (PATHS, D, D), jnp.float32) ** level_of(splits[6], (PATHS, D, D), ((0, 64), (2, 16)), -0.2, 0.2)), 0.0099487305, 1.0).astype(jnp.bfloat16),
        "master_weights": noise(splits[7], (MODULES, D, D), 1.0, 5.0, ((1, 64), (2, 16)), jnp.float32),
        "outer_momentum": noise(splits[8], (MODULES, D, D), 0.5, 3.0, ((1, 64), (2, 16)), jnp.float32),
    }


beta_first = 0.9
beta_second = 0.95
inner_rate = 0.05
decay_rate = 0.1
epsilon = 1e-08
nesterov = 0.9
outer_rate = 0.7

def reference(token_pool, batch_ids, module_table, cotangent, path_weights, first_moment, second_moment, master_weights, outer_momentum):
    factor = D ** (-0.5)

    def visit_path(totals, inputs):
        token_ids, cot_rows, weights, first_old, second_old, module = inputs
        tokens = jnp.take(token_pool, token_ids, axis=0)
        pre_act = jnp.dot(tokens, weights, preferred_element_type=jnp.float32) * factor
        sigmoid_act = jax.nn.sigmoid(pre_act)
        slope = (cot_rows.astype(jnp.float32) * sigmoid_act * (1.0 + pre_act * (1.0 - sigmoid_act))).astype(jnp.bfloat16)
        gradient = jnp.dot(tokens.T, slope, preferred_element_type=jnp.float32) * factor
        moment_one = beta_first * first_old.astype(jnp.float32) + (1.0 - beta_first) * gradient
        moment_two = beta_second * second_old.astype(jnp.float32) + (1.0 - beta_second) * gradient * gradient
        weights_old = weights.astype(jnp.float32)
        weights_new = weights_old - inner_rate * (moment_one / (jnp.sqrt(moment_two) + epsilon) + decay_rate * weights_old)
        sum_weights, sum_first, sum_second = totals
        sum_weights = sum_weights.at[module].add(lax.optimization_barrier(weights_new.astype(jnp.bfloat16)).astype(jnp.float32))
        sum_first = sum_first.at[module].add(lax.optimization_barrier(moment_one.astype(jnp.bfloat16)).astype(jnp.float32))
        sum_second = sum_second.at[module].add(lax.optimization_barrier(moment_two.astype(jnp.bfloat16)).astype(jnp.float32))
        return ((sum_weights, sum_first, sum_second), None)
    empty = jnp.zeros((MODULES, D, D), jnp.float32)
    totals, _ = lax.scan(visit_path, (empty, empty, empty), (batch_ids, cotangent, path_weights, first_moment, second_moment, module_table))
    sum_weights, sum_first, sum_second = totals
    labels = jnp.arange(MODULES, dtype=jnp.int32)
    counts = lax.optimization_barrier(jnp.sum((module_table[None, :] == labels[:, None]).astype(jnp.int32), axis=1))
    divisor = jnp.maximum(counts, 1).astype(jnp.float32)[:, None, None]
    used = (counts > 0)[:, None, None]
    delta = jnp.where(used, master_weights - sum_weights / divisor, jnp.zeros_like(master_weights))
    first_average = (sum_first / divisor).astype(jnp.bfloat16)
    second_average = (sum_second / divisor).astype(jnp.bfloat16)
    new_momentum = nesterov * outer_momentum + delta
    new_master = master_weights - outer_rate * (delta + nesterov * new_momentum)
    return (new_master, new_momentum, first_average, second_average)
```

```python
import jax
import jax.numpy as jnp
from jax import lax
from jax.experimental import pallas as pl
from jax.experimental.pallas import tpu as pltpu
from jax.sharding import Mesh
from jax.sharding import PartitionSpec as P

beta_first = 0.9
beta_second = 0.95
inner_rate = 0.05
decay_rate = 0.1
epsilon = 1e-08
nesterov = 0.9
outer_rate = 0.7

MIB = 1 << 20


def split_bf16(values):
    high = values.astype(jnp.bfloat16)
    low = (values - high.astype(jnp.float32)).astype(jnp.bfloat16)
    return high, low


def gradient_kernel(
    core, near, far, onehot, cotangent, weights, first_old, second_old, sent
):
    stations, pool, width = near.shape
    features = 2 * stations * width
    factor = features ** (-0.5)
    mine = core[0]
    pools = []
    product = None
    for held, side in ((near, mine), (far, 1 - mine)):
        rows = jnp.concatenate([held[s] for s in range(stations)], axis=1)
        block = jnp.concatenate([weights[s, side] for s in range(stations)], axis=0)
        part = jnp.dot(rows, block, preferred_element_type=jnp.float32)
        product = part if product is None else product + part
        pools.append(rows)
    both = jnp.concatenate(split_bf16(product * factor), axis=1)
    taken = jnp.dot(onehot[...], both, preferred_element_type=jnp.float32)
    pre_act = taken[:, :width] + taken[:, width:]
    gate = 1.0 / (1.0 + jnp.exp(-pre_act))
    slope = cotangent[...].astype(jnp.float32) * gate * (1.0 + pre_act * (1.0 - gate))
    slope = slope.astype(jnp.bfloat16)
    summed = lax.dot_general(
        slope, onehot[...], (((0,), (0,)), ((), ())), preferred_element_type=jnp.float32
    )
    pair = jnp.concatenate(split_bf16(summed), axis=0)
    for rows, side in zip(pools, (mine, 1 - mine)):
        both = jnp.dot(pair, rows, preferred_element_type=jnp.float32)
        gradient = (both[:width] + both[width:]) * factor
        for s in range(stations):
            block = jnp.transpose(gradient[:, s * width : (s + 1) * width])
            first = first_old[s, side].astype(jnp.float32)
            first = beta_first * first + (1.0 - beta_first) * block
            second = second_old[s, side].astype(jnp.float32)
            second = beta_second * second + (1.0 - beta_second) * block * block
            rows_own = sent.shape[3] // 2
            for part in range(sent.shape[2]):
                at = slice(part * rows_own, (part + 1) * rows_own)
                sent[s, side, part, :rows_own] = first[at].astype(jnp.bfloat16)
                sent[s, side, part, rows_own:] = second[at].astype(jnp.bfloat16)


def module_kernel(
    table, early, late, master, momentum, new_master, new_momentum, first_out, second_out, totals, counts
):
    paths = late.shape[0]
    modules, rows, _ = master.shape
    totals[...] = jnp.zeros_like(totals)

    def clear(k, carry):
        counts[k] = 0
        return carry

    lax.fori_loop(0, modules, clear, 0)

    def visit(p, carry):
        module = table[p]
        counts[module] = counts[module] + 1
        old = early[p].astype(jnp.float32)
        first = late[p, 0:rows].astype(jnp.float32)
        second = late[p, rows : 2 * rows].astype(jnp.float32)
        new = old - inner_rate * (first / (jnp.sqrt(second) + epsilon) + decay_rate * old)
        totals[0, module] += new.astype(jnp.bfloat16).astype(jnp.float32)
        totals[1, module] += first
        totals[2, module] += second
        return carry

    lax.fori_loop(0, paths, visit, 0, unroll=4)

    def finish(k, carry):
        count = counts[k]
        divisor = jnp.maximum(count, 1).astype(jnp.float32)
        old = master[k]
        delta = jnp.where(count > 0, old - totals[0, k] / divisor, jnp.zeros_like(old))
        moved = nesterov * momentum[k] + delta
        new_momentum[k] = moved
        new_master[k] = old - outer_rate * (delta + nesterov * moved)
        first_out[k] = (totals[1, k] / divisor).astype(jnp.bfloat16)
        second_out[k] = (totals[2, k] / divisor).astype(jnp.bfloat16)
        return carry

    lax.fori_loop(0, modules, finish, 0)


def whole(count):
    return [pl.BlockSpec(memory_space=pltpu.VMEM) for _ in range(count)]


def per_device(
    token_pool,
    batch_ids,
    module_table,
    cotangent,
    path_weights,
    first_moment,
    second_moment,
    master_weights,
    outer_momentum,
):
    stations = lax.axis_size("y")
    groups = lax.axis_size("z") * lax.axis_size("x")
    pool, width = token_pool.shape
    features = path_weights.shape[1]
    rows = features // groups
    tokens = batch_ids.shape[1]
    path_axes = ("z", "x")

    near = lax.all_to_all(
        jnp.broadcast_to(token_pool[None], (stations, pool, width)), "y", 0, 0, tiled=True
    )
    far = lax.ppermute(near, "core", [(0, 1), (1, 0)])

    early = lax.all_to_all(
        path_weights[0].reshape(groups, rows, width), path_axes, 0, 0, tiled=True
    )

    onehot = (
        batch_ids[0][:, None] == lax.broadcasted_iota(jnp.int32, (tokens, pool), 1)
    ).astype(jnp.bfloat16)
    core = lax.axis_index("core").astype(jnp.int32).reshape(1)

    sent = pl.pallas_call(
        gradient_kernel,
        out_shape=jax.ShapeDtypeStruct(
            (stations, 2, width // rows, 2 * rows, width), jnp.bfloat16
        ),
        in_specs=[pl.BlockSpec(memory_space=pltpu.SMEM)] + whole(7),
        out_specs=pl.BlockSpec(memory_space=pltpu.VMEM),
        compiler_params=pltpu.CompilerParams(vmem_limit_bytes=32 * MIB),
        cost_estimate=pl.CostEstimate(
            flops=2_000_000_000, bytes_accessed=5 * MIB, transcendentals=tokens * width
        ),
        name="path_gradient",
    )(
        core,
        near,
        far,
        onehot,
        cotangent[0],
        path_weights[0].reshape(stations, 2, width, width),
        first_moment[0].reshape(stations, 2, width, width),
        second_moment[0].reshape(stations, 2, width, width),
    )

    late = lax.all_to_all(sent.reshape(groups, 2 * rows, width), path_axes, 0, 0, tiled=True)

    shape = master_weights.shape
    return pl.pallas_call(
        module_kernel,
        out_shape=(
            jax.ShapeDtypeStruct(shape, jnp.float32),
            jax.ShapeDtypeStruct(shape, jnp.float32),
            jax.ShapeDtypeStruct(shape, jnp.bfloat16),
            jax.ShapeDtypeStruct(shape, jnp.bfloat16),
        ),
        in_specs=[pl.BlockSpec(memory_space=pltpu.SMEM)] + whole(4),
        out_specs=tuple(whole(4)),
        scratch_shapes=[
            pltpu.VMEM((3,) + shape, jnp.float32),
            pltpu.SMEM((shape[0],), jnp.int32),
        ],
        compiler_params=pltpu.CompilerParams(vmem_limit_bytes=32 * MIB),
        cost_estimate=pl.CostEstimate(
            flops=10_000_000, bytes_accessed=4 * MIB, transcendentals=4 * groups * rows * width
        ),
        name="module_update",
    )(module_table, early, late, master_weights, outer_momentum)


def solution(mesh):
    lengths = (8, 8, 8, 2)
    split = Mesh(mesh.devices.reshape(lengths), ("z", "x", "y", "core"))
    path = ("z", "x")
    fsdp = ("y", "core")
    in_specs = (
        P(None, fsdp),
        P(path, None),
        P(),
        P(path, None, fsdp),
        P(path, None, fsdp),
        P(path, None, fsdp),
        P(path, None, fsdp),
        P(None, path, fsdp),
        P(None, path, fsdp),
    )
    out_specs = (P(None, path, fsdp),) * 4
    return jax.shard_map(
        per_device, mesh=split, in_specs=in_specs, out_specs=out_specs, check_vma=False
    )
```

```python
import jax
import jax.numpy as jnp
from jax import lax
from jax.experimental import pallas as pl
from jax.experimental.pallas import tpu as pltpu
from jax.sharding import Mesh
from jax.sharding import PartitionSpec as P

beta_first = 0.9
beta_second = 0.95
inner_rate = 0.05
decay_rate = 0.1
epsilon = 1e-08
nesterov = 0.9
outer_rate = 0.7

MIB = 1 << 20
CHUNKS = 4


def split_bf16(values):
    high = values.astype(jnp.bfloat16)
    low = (values - high.astype(jnp.float32)).astype(jnp.bfloat16)
    return high, low


def gradient_kernel(
    place, chip_held, near, far, onehot, cotangent_held, weights, sent, chip, cotangent, arrived
):
    chip_copy = pltpu.make_async_copy(chip_held, chip, arrived.at[0])
    cotangent_copy = pltpu.make_async_copy(cotangent_held, cotangent, arrived.at[1])
    chip_copy.start()
    cotangent_copy.start()
    _, pool, width = chip.shape
    stations = weights.shape[0]
    factor = (2 * stations * width) ** (-0.5)
    spot, core = place[0], place[1]
    step = 2 * core - 1
    half = pool // 2
    opposite = lax.rem(spot + stations // 2, stations)
    chip_copy.wait()
    slices = [(chip[0], spot, core), (chip[1], spot, 1 - core)]
    for held, way, first in ((near, step, core), (far, -step, 1 - core)):
        for hop in range(1, stations // 2):
            at = lax.rem(spot + hop * way + stations, stations)
            for index, side in enumerate((first, 1 - first)):
                start = (2 * (hop - 1) + index) * pool
                slices.append((held[start : start + pool], at, side))
    start = 2 * (stations // 2 - 1) * pool
    mine = [near[start + i * half : start + (i + 1) * half] for i in range(2)]
    other = [far[start + i * half : start + (i + 1) * half] for i in range(2)]
    low = core == 0
    for index, side in enumerate((core, 1 - core)):
        here, there = mine[index], other[1 - index]
        rows = jnp.concatenate(
            [jnp.where(low, here, there), jnp.where(low, there, here)], axis=0
        )
        slices.append((rows, opposite, side))
    rows = jnp.concatenate([part for part, _, _ in slices], axis=1)
    block = jnp.concatenate([weights[at, side] for _, at, side in slices], axis=0)
    product = jnp.dot(rows, block, preferred_element_type=jnp.float32) * factor
    both = jnp.concatenate(split_bf16(product), axis=1)
    taken = jnp.dot(onehot[...], both, preferred_element_type=jnp.float32)
    pre_act = taken[:, :width] + taken[:, width:]
    gate = 1.0 / (1.0 + jnp.exp(-pre_act))
    cotangent_copy.wait()
    slope = cotangent[...].astype(jnp.float32) * gate * (1.0 + pre_act * (1.0 - gate))
    slope = slope.astype(jnp.bfloat16)
    summed = lax.dot_general(
        slope, onehot[...], (((0,), (0,)), ((), ())), preferred_element_type=jnp.float32
    )
    pair = jnp.concatenate(split_bf16(summed), axis=0)
    both = jnp.dot(pair, rows, preferred_element_type=jnp.float32)
    gradient = (both[:width] + both[width:]) * factor
    signed = gradient * jnp.abs(gradient)
    for index, (_, at, side) in enumerate(slices):
        values = jnp.transpose(signed[:, index * width : (index + 1) * width])
        sent[at, side] = values.astype(jnp.bfloat16)


def module_kernel(
    table,
    early_held,
    late_held,
    master_held,
    momentum_held,
    new_master,
    new_momentum,
    first_out,
    second_out,
    totals,
    counts,
    early,
    late,
    master,
    momentum,
    arrived,
):
    paths = late.shape[0]
    modules, rows, _ = master.shape
    span = paths // CHUNKS
    pairs = []
    for chunk in range(CHUNKS):
        at = pl.ds(chunk * span, span)
        pairs.append((early_held.at[at], early.at[at]))
        pairs.append((late_held.at[at], late.at[at]))
    pairs += [(master_held, master), (momentum_held, momentum)]
    copies = [
        pltpu.make_async_copy(held, here, arrived.at[i]) for i, (held, here) in enumerate(pairs)
    ]
    for copy in copies:
        copy.start()
    totals[...] = jnp.zeros_like(totals)

    def clear(k, carry):
        counts[k] = 0
        return carry

    lax.fori_loop(0, modules, clear, 0)

    def visit(p, carry):
        module = table[p]
        counts[module] = counts[module] + 1
        signed = late[p].astype(jnp.float32)
        size = jnp.abs(signed)
        root = jnp.sqrt(size)
        gradient = jnp.where(signed < 0.0, -root, root)
        old = early[p, 0:rows].astype(jnp.float32)
        first = early[p, rows : 2 * rows].astype(jnp.float32)
        second = early[p, 2 * rows : 3 * rows].astype(jnp.float32)
        first = beta_first * first + (1.0 - beta_first) * gradient
        second = beta_second * second + (1.0 - beta_second) * size
        new = old - inner_rate * (first / (jnp.sqrt(second) + epsilon) + decay_rate * old)
        for index, values in enumerate((new, first, second)):
            totals[index, module] += values.astype(jnp.bfloat16).astype(jnp.float32)
        return carry

    for chunk in range(CHUNKS):
        copies[2 * chunk].wait()
        copies[2 * chunk + 1].wait()
        lax.fori_loop(chunk * span, (chunk + 1) * span, visit, 0, unroll=4)
    for copy in copies[2 * CHUNKS :]:
        copy.wait()

    def finish(k, carry):
        count = counts[k]
        divisor = jnp.maximum(count, 1).astype(jnp.float32)
        old = master[k]
        delta = jnp.where(count > 0, old - totals[0, k] / divisor, jnp.zeros_like(old))
        moved = nesterov * momentum[k] + delta
        new_momentum[k] = moved
        new_master[k] = old - outer_rate * (delta + nesterov * moved)
        first_out[k] = (totals[1, k] / divisor).astype(jnp.bfloat16)
        second_out[k] = (totals[2, k] / divisor).astype(jnp.bfloat16)
        return carry

    lax.fori_loop(0, modules, finish, 0)


def whole(count):
    return [pl.BlockSpec(memory_space=pltpu.VMEM) for _ in range(count)]


def in_hbm(count):
    return [pl.BlockSpec(memory_space=pltpu.HBM) for _ in range(count)]


def per_device(
    token_pool,
    batch_ids,
    module_table,
    cotangent,
    path_weights,
    first_moment,
    second_moment,
    master_weights,
    outer_momentum,
):
    stations = lax.axis_size("y")
    groups = lax.axis_size("z") * lax.axis_size("x")
    pool, width = token_pool.shape
    features = path_weights.shape[1]
    rows = features // groups
    tokens = batch_ids.shape[1]
    path_axes = ("z", "x")

    fsdp_axes = ("y", "core")
    spot, core = lax.axis_index("y"), lax.axis_index("core")

    def swap(values):
        return lax.ppermute(values, "core", [(0, 1), (1, 0)])

    def hop(values, by):
        ways = [(2 * i, 2 * ((i + by) % stations)) for i in range(stations)]
        ways += [(2 * i + 1, 2 * ((i - by) % stations) + 1) for i in range(stations)]
        return lax.ppermute(values, fsdp_axes, ways)

    packed = jnp.concatenate(
        [v[0].reshape(groups, rows, width) for v in (path_weights, first_moment, second_moment)],
        axis=1,
    )
    chip = jnp.stack([token_pool, swap(token_pool)])
    chip, packed = lax.optimization_barrier((chip, packed))
    half = pool // 2
    held = {1: hop(chip, 1), 2: hop(chip, 2)}
    held[3] = hop(held[1], 2)
    held[4] = hop(lax.dynamic_slice_in_dim(held[2], core * half, half, axis=1), 2)
    near = jnp.concatenate([held[by].reshape(-1, width) for by in sorted(held)])
    far = swap(near)

    early = lax.all_to_all(packed, path_axes, 0, 0, tiled=True)

    onehot = (
        batch_ids[0][:, None] == lax.broadcasted_iota(jnp.int32, (tokens, pool), 1)
    ).astype(jnp.bfloat16)
    place = jnp.stack([spot, core]).astype(jnp.int32)

    sent = pl.pallas_call(
        gradient_kernel,
        out_shape=jax.ShapeDtypeStruct((stations, 2, width, width), jnp.bfloat16),
        in_specs=[pl.BlockSpec(memory_space=pltpu.SMEM)]
        + in_hbm(1)
        + whole(3)
        + in_hbm(1)
        + whole(1),
        out_specs=pl.BlockSpec(memory_space=pltpu.VMEM),
        scratch_shapes=[
            pltpu.VMEM((2, pool, width), jnp.bfloat16),
            pltpu.VMEM((tokens, width), jnp.bfloat16),
            pltpu.SemaphoreType.DMA((2,)),
        ],
        compiler_params=pltpu.CompilerParams(vmem_limit_bytes=20 * MIB),
        cost_estimate=pl.CostEstimate(
            flops=2_000_000_000, bytes_accessed=5 * MIB, transcendentals=tokens * width
        ),
        name="path_gradient",
    )(place, chip, near, far, onehot, cotangent[0], path_weights[0].reshape(stations, 2, width, width))

    sent, early = lax.optimization_barrier((sent, early))
    late = lax.all_to_all(sent.reshape(groups, rows, width), path_axes, 0, 0, tiled=True)

    shape = master_weights.shape
    return pl.pallas_call(
        module_kernel,
        out_shape=(
            jax.ShapeDtypeStruct(shape, jnp.float32),
            jax.ShapeDtypeStruct(shape, jnp.float32),
            jax.ShapeDtypeStruct(shape, jnp.bfloat16),
            jax.ShapeDtypeStruct(shape, jnp.bfloat16),
        ),
        in_specs=[pl.BlockSpec(memory_space=pltpu.SMEM)] + in_hbm(4),
        out_specs=tuple(whole(4)),
        scratch_shapes=[
            pltpu.VMEM((3,) + shape, jnp.float32),
            pltpu.SMEM((shape[0],), jnp.int32),
            pltpu.VMEM((groups, 3 * rows, width), jnp.bfloat16),
            pltpu.VMEM((groups, rows, width), jnp.bfloat16),
            pltpu.VMEM(shape, jnp.float32),
            pltpu.VMEM(shape, jnp.float32),
            pltpu.SemaphoreType.DMA((2 * CHUNKS + 2,)),
        ],
        compiler_params=pltpu.CompilerParams(vmem_limit_bytes=56 * MIB),
        cost_estimate=pl.CostEstimate(
            flops=10_000_000, bytes_accessed=4 * MIB, transcendentals=4 * groups * rows * width
        ),
        name="module_update",
    )(module_table, early, late, master_weights, outer_momentum)


def solution(mesh):
    lengths = (8, 8, 8, 2)
    split = Mesh(mesh.devices.reshape(lengths), ("z", "x", "y", "core"))
    path = ("z", "x")
    fsdp = ("y", "core")
    in_specs = (
        P(None, fsdp),
        P(path, None),
        P(),
        P(path, None, fsdp),
        P(path, None, fsdp),
        P(path, None, fsdp),
        P(path, None, fsdp),
        P(None, path, fsdp),
        P(None, path, fsdp),
    )
    out_specs = (P(None, path, fsdp),) * 4
    return jax.shard_map(
        per_device, mesh=split, in_specs=in_specs, out_specs=out_specs, check_vma=False
    )
```

```python
import jax
import jax.numpy as jnp
from jax import lax
from jax.experimental import pallas as pl
from jax.experimental.pallas import tpu as pltpu
from jax.sharding import Mesh
from jax.sharding import PartitionSpec as P

beta_first = 0.9
beta_second = 0.95
inner_rate = 0.05
decay_rate = 0.1
epsilon = 1e-08
nesterov = 0.9
outer_rate = 0.7

MIB = 1 << 20
CHUNKS = 4
TINY = 1e-36


def split_bf16(values):
    high = values.astype(jnp.bfloat16)
    low = (values - high.astype(jnp.float32)).astype(jnp.bfloat16)
    return high, low


def pack_kernel(weights, first, second, packed, held, arrived, left):
    groups, rows, _ = weights.shape
    span = groups // CHUNKS
    parts = [pl.ds(chunk * span, span) for chunk in range(CHUNKS)]
    inward = [
        [
            pltpu.make_async_copy(
                part.at[at], held.at[at, pl.ds(i * rows, rows)], arrived.at[chunk, i]
            )
            for i, part in enumerate((weights, first, second))
        ]
        for chunk, at in enumerate(parts)
    ]
    outward = [
        pltpu.make_async_copy(held.at[at], packed.at[at], left.at[chunk])
        for chunk, at in enumerate(parts)
    ]
    for copies in inward:
        for copy in copies:
            copy.start()
    for copies, away in zip(inward, outward):
        for copy in copies:
            copy.wait()
        away.start()
    for away in outward:
        away.wait()


def gradient_kernel(
    place, chip_held, near, far, onehot, cotangent_held, weights, sent, chip, cotangent, arrived
):
    chip_copy = pltpu.make_async_copy(chip_held, chip, arrived.at[0])
    cotangent_copy = pltpu.make_async_copy(cotangent_held, cotangent, arrived.at[1])
    chip_copy.start()
    cotangent_copy.start()
    _, pool, width = chip.shape
    stations = weights.shape[0]
    factor = (2 * stations * width) ** (-0.5)
    spot, core = place[0], place[1]
    step = 2 * core - 1
    half = pool // 2
    opposite = lax.rem(spot + stations // 2, stations)
    chip_copy.wait()
    slices = [(chip[0], spot, core), (chip[1], spot, 1 - core)]
    for held, way, first in ((near, step, core), (far, -step, 1 - core)):
        for hop in range(1, stations // 2):
            at = lax.rem(spot + hop * way + stations, stations)
            for index, side in enumerate((first, 1 - first)):
                start = (2 * (hop - 1) + index) * pool
                slices.append((held[start : start + pool], at, side))
    start = 2 * (stations // 2 - 1) * pool
    mine = [near[start + i * half : start + (i + 1) * half] for i in range(2)]
    other = [far[start + i * half : start + (i + 1) * half] for i in range(2)]
    low = core == 0
    for index, side in enumerate((core, 1 - core)):
        here, there = mine[index], other[1 - index]
        rows = jnp.concatenate(
            [jnp.where(low, here, there), jnp.where(low, there, here)], axis=0
        )
        slices.append((rows, opposite, side))
    rows = jnp.concatenate([part for part, _, _ in slices], axis=1)
    block = jnp.concatenate([weights[at, side] for _, at, side in slices], axis=0)
    product = jnp.dot(rows, block, preferred_element_type=jnp.float32) * factor
    both = jnp.concatenate(split_bf16(product), axis=1)
    taken = jnp.dot(onehot[...], both, preferred_element_type=jnp.float32)
    pre_act = taken[:, :width] + taken[:, width:]
    gate = 1.0 / (1.0 + jnp.exp(-pre_act))
    cotangent_copy.wait()
    slope = cotangent[...].astype(jnp.float32) * gate * (1.0 + pre_act * (1.0 - gate))
    slope = slope.astype(jnp.bfloat16)
    summed = lax.dot_general(
        slope, onehot[...], (((0,), (0,)), ((), ())), preferred_element_type=jnp.float32
    )
    pair = jnp.concatenate(split_bf16(summed), axis=0)
    both = jnp.dot(pair, rows, preferred_element_type=jnp.float32)
    gradient = (both[:width] + both[width:]) * factor
    signed = gradient * jnp.abs(gradient)
    for index, (_, at, side) in enumerate(slices):
        values = jnp.transpose(signed[:, index * width : (index + 1) * width])
        sent[at, side] = values.astype(jnp.bfloat16)


def module_kernel(
    table,
    early_held,
    late_held,
    master_held,
    momentum_held,
    new_master,
    new_momentum,
    first_out,
    second_out,
    totals,
    counts,
    early,
    late,
    master,
    momentum,
    arrived,
):
    paths = late.shape[0]
    modules, rows, _ = master.shape
    span = paths // CHUNKS
    pairs = []
    for chunk in range(CHUNKS):
        at = pl.ds(chunk * span, span)
        pairs.append((early_held.at[at], early.at[at]))
        pairs.append((late_held.at[at], late.at[at]))
    pairs += [(master_held, master), (momentum_held, momentum)]
    copies = [
        pltpu.make_async_copy(held, here, arrived.at[i]) for i, (held, here) in enumerate(pairs)
    ]
    for copy in copies:
        copy.start()
    totals[...] = jnp.zeros_like(totals)

    def clear(k, carry):
        counts[k] = 0
        return carry

    lax.fori_loop(0, modules, clear, 0)

    def visit(p, carry):
        module = table[p]
        counts[module] = counts[module] + 1
        signed = late[p].astype(jnp.float32)
        size = jnp.abs(signed)
        gradient = signed * lax.rsqrt(jnp.maximum(size, TINY))
        old = early[p, 0:rows].astype(jnp.float32)
        first = early[p, rows : 2 * rows].astype(jnp.float32)
        second = early[p, 2 * rows : 3 * rows].astype(jnp.float32)
        first = beta_first * first + (1.0 - beta_first) * gradient
        second = beta_second * second + (1.0 - beta_second) * size
        root = second * lax.rsqrt(second)
        new = old - inner_rate * (first / (root + epsilon) + decay_rate * old)
        for index, values in enumerate((new, first, second)):
            totals[index, module] += values.astype(jnp.bfloat16).astype(jnp.float32)
        return carry

    for chunk in range(CHUNKS):
        copies[2 * chunk].wait()
        copies[2 * chunk + 1].wait()
        lax.fori_loop(chunk * span, (chunk + 1) * span, visit, 0, unroll=8)
    for copy in copies[2 * CHUNKS :]:
        copy.wait()

    def finish(k, carry):
        count = counts[k]
        divisor = jnp.maximum(count, 1).astype(jnp.float32)
        old = master[k]
        delta = jnp.where(count > 0, old - totals[0, k] / divisor, jnp.zeros_like(old))
        moved = nesterov * momentum[k] + delta
        new_momentum[k] = moved
        new_master[k] = old - outer_rate * (delta + nesterov * moved)
        first_out[k] = (totals[1, k] / divisor).astype(jnp.bfloat16)
        second_out[k] = (totals[2, k] / divisor).astype(jnp.bfloat16)
        return carry

    lax.fori_loop(0, modules, finish, 0, unroll=4)


def whole(count):
    return [pl.BlockSpec(memory_space=pltpu.VMEM) for _ in range(count)]


def in_hbm(count):
    return [pl.BlockSpec(memory_space=pltpu.HBM) for _ in range(count)]


def per_device(
    token_pool,
    batch_ids,
    module_table,
    cotangent,
    path_weights,
    first_moment,
    second_moment,
    master_weights,
    outer_momentum,
):
    stations = lax.axis_size("y")
    groups = lax.axis_size("z") * lax.axis_size("x")
    pool, width = token_pool.shape
    features = path_weights.shape[1]
    rows = features // groups
    tokens = batch_ids.shape[1]
    path_axes = ("z", "x")

    fsdp_axes = ("y", "core")
    spot, core = lax.axis_index("y"), lax.axis_index("core")

    def swap(values):
        return lax.ppermute(values, "core", [(0, 1), (1, 0)])

    def hop(values, by):
        ways = [(2 * i, 2 * ((i + by) % stations)) for i in range(stations)]
        ways += [(2 * i + 1, 2 * ((i - by) % stations) + 1) for i in range(stations)]
        return lax.ppermute(values, fsdp_axes, ways)

    packed = pl.pallas_call(
        pack_kernel,
        out_shape=jax.ShapeDtypeStruct((groups, 3 * rows, width), jnp.bfloat16),
        in_specs=in_hbm(3),
        out_specs=pl.BlockSpec(memory_space=pltpu.HBM),
        scratch_shapes=[
            pltpu.VMEM((groups, 3 * rows, width), jnp.bfloat16),
            pltpu.SemaphoreType.DMA((CHUNKS, 3)),
            pltpu.SemaphoreType.DMA((CHUNKS,)),
        ],
        compiler_params=pltpu.CompilerParams(vmem_limit_bytes=56 * MIB),
        cost_estimate=pl.CostEstimate(flops=0, bytes_accessed=3 * MIB, transcendentals=0),
        name="pack",
    )(*[v[0].reshape(groups, rows, width) for v in (path_weights, first_moment, second_moment)])

    chip = jnp.stack([token_pool, swap(token_pool)])
    chip, packed = lax.optimization_barrier((chip, packed))
    half = pool // 2
    held = {1: hop(chip, 1), 2: hop(chip, 2)}
    held[3] = hop(held[1], 2)
    held[4] = hop(lax.dynamic_slice_in_dim(held[2], core * half, half, axis=1), 2)
    near = jnp.concatenate([held[by].reshape(-1, width) for by in sorted(held)])
    far = swap(near)

    early = lax.all_to_all(packed, path_axes, 0, 0, tiled=True)

    onehot = (
        batch_ids[0][:, None] == lax.broadcasted_iota(jnp.int32, (tokens, pool), 1)
    ).astype(jnp.bfloat16)
    place = jnp.stack([spot, core]).astype(jnp.int32)

    sent = pl.pallas_call(
        gradient_kernel,
        out_shape=jax.ShapeDtypeStruct((stations, 2, width, width), jnp.bfloat16),
        in_specs=[pl.BlockSpec(memory_space=pltpu.SMEM)]
        + in_hbm(1)
        + whole(3)
        + in_hbm(1)
        + whole(1),
        out_specs=pl.BlockSpec(memory_space=pltpu.VMEM),
        scratch_shapes=[
            pltpu.VMEM((2, pool, width), jnp.bfloat16),
            pltpu.VMEM((tokens, width), jnp.bfloat16),
            pltpu.SemaphoreType.DMA((2,)),
        ],
        compiler_params=pltpu.CompilerParams(vmem_limit_bytes=20 * MIB),
        cost_estimate=pl.CostEstimate(
            flops=2_000_000_000, bytes_accessed=5 * MIB, transcendentals=tokens * width
        ),
        name="path_gradient",
    )(place, chip, near, far, onehot, cotangent[0], path_weights[0].reshape(stations, 2, width, width))

    sent, early = lax.optimization_barrier((sent, early))
    late = lax.all_to_all(sent.reshape(groups, rows, width), path_axes, 0, 0, tiled=True)

    shape = master_weights.shape
    return pl.pallas_call(
        module_kernel,
        out_shape=(
            jax.ShapeDtypeStruct(shape, jnp.float32),
            jax.ShapeDtypeStruct(shape, jnp.float32),
            jax.ShapeDtypeStruct(shape, jnp.bfloat16),
            jax.ShapeDtypeStruct(shape, jnp.bfloat16),
        ),
        in_specs=[pl.BlockSpec(memory_space=pltpu.SMEM)] + in_hbm(4),
        out_specs=tuple(whole(4)),
        scratch_shapes=[
            pltpu.VMEM((3,) + shape, jnp.float32),
            pltpu.SMEM((shape[0],), jnp.int32),
            pltpu.VMEM((groups, 3 * rows, width), jnp.bfloat16),
            pltpu.VMEM((groups, rows, width), jnp.bfloat16),
            pltpu.VMEM(shape, jnp.float32),
            pltpu.VMEM(shape, jnp.float32),
            pltpu.SemaphoreType.DMA((2 * CHUNKS + 2,)),
        ],
        compiler_params=pltpu.CompilerParams(vmem_limit_bytes=56 * MIB),
        cost_estimate=pl.CostEstimate(
            flops=10_000_000, bytes_accessed=4 * MIB, transcendentals=4 * groups * rows * width
        ),
        name="module_update",
    )(module_table, early, late, master_weights, outer_momentum)


def solution(mesh):
    lengths = (8, 8, 8, 2)
    split = Mesh(mesh.devices.reshape(lengths), ("z", "x", "y", "core"))
    path = ("z", "x")
    fsdp = ("y", "core")
    in_specs = (
        P(None, fsdp),
        P(path, None),
        P(),
        P(path, None, fsdp),
        P(path, None, fsdp),
        P(path, None, fsdp),
        P(path, None, fsdp),
        P(None, path, fsdp),
        P(None, path, fsdp),
    )
    out_specs = (P(None, path, fsdp),) * 4
    return jax.shard_map(
        per_device, mesh=split, in_specs=in_specs, out_specs=out_specs, check_vma=False
    )
```

```python
import jax
import jax.numpy as jnp
from jax import lax
from jax.experimental import pallas as pl
from jax.experimental.pallas import tpu as pltpu
from jax.sharding import Mesh
from jax.sharding import PartitionSpec as P

beta_first = 0.9
beta_second = 0.95
inner_rate = 0.05
decay_rate = 0.1
epsilon = 1e-08
nesterov = 0.9
outer_rate = 0.7

MIB = 1 << 20
CHUNKS = 8
TINY = 1e-36


def split_bf16(values):
    high = values.astype(jnp.bfloat16)
    low = (values - high.astype(jnp.float32)).astype(jnp.bfloat16)
    return high, low


def pack_kernel(weights, first, second, packed, held, arrived, left):
    groups, rows, _ = weights.shape
    span = groups // CHUNKS
    parts = [pl.ds(chunk * span, span) for chunk in range(CHUNKS)]
    inward = [
        [
            pltpu.make_async_copy(
                part.at[at], held.at[at, pl.ds(i * rows, rows)], arrived.at[chunk, i]
            )
            for i, part in enumerate((weights, first, second))
        ]
        for chunk, at in enumerate(parts)
    ]
    outward = [
        pltpu.make_async_copy(held.at[at], packed.at[at], left.at[chunk])
        for chunk, at in enumerate(parts)
    ]
    for copies in inward:
        for copy in copies:
            copy.start()
    for copies, away in zip(inward, outward):
        for copy in copies:
            copy.wait()
        away.start()
    for away in outward:
        away.wait()


def gradient_kernel(place, chip, near, far, onehot, cotangent, weights, sent):
    _, pool, width = chip.shape
    stations = weights.shape[0]
    factor = (2 * stations * width) ** (-0.5)
    spot, core = place[0], place[1]
    step = 2 * core - 1
    half = pool // 2
    opposite = lax.rem(spot + stations // 2, stations)
    slices = [(chip[0], spot, core), (chip[1], spot, 1 - core)]
    for held, way, first in ((near, step, core), (far, -step, 1 - core)):
        for hop in range(1, stations // 2):
            at = lax.rem(spot + hop * way + stations, stations)
            for index, side in enumerate((first, 1 - first)):
                start = (2 * (hop - 1) + index) * pool
                slices.append((held[start : start + pool], at, side))
    start = 2 * (stations // 2 - 1) * pool
    mine = [near[start + i * half : start + (i + 1) * half] for i in range(2)]
    other = [far[start + i * half : start + (i + 1) * half] for i in range(2)]
    low = core == 0
    for index, side in enumerate((core, 1 - core)):
        here, there = mine[index], other[1 - index]
        rows = jnp.concatenate(
            [jnp.where(low, here, there), jnp.where(low, there, here)], axis=0
        )
        slices.append((rows, opposite, side))
    rows = jnp.concatenate([part for part, _, _ in slices], axis=1)
    block = jnp.concatenate([weights[at, side] for _, at, side in slices], axis=0)
    product = jnp.dot(rows, block, preferred_element_type=jnp.float32) * factor
    both = jnp.concatenate(split_bf16(product), axis=1)
    taken = jnp.dot(onehot[...], both, preferred_element_type=jnp.float32)
    pre_act = taken[:, :width] + taken[:, width:]
    gate = 1.0 / (1.0 + jnp.exp(-pre_act))
    slope = cotangent[...].astype(jnp.float32) * gate * (1.0 + pre_act * (1.0 - gate))
    slope = slope.astype(jnp.bfloat16)
    summed = lax.dot_general(
        slope, onehot[...], (((0,), (0,)), ((), ())), preferred_element_type=jnp.float32
    )
    pair = jnp.concatenate(split_bf16(summed), axis=0)
    both = jnp.dot(pair, rows, preferred_element_type=jnp.float32)
    gradient = (both[:width] + both[width:]) * factor
    signed = gradient * jnp.abs(gradient)
    for index, (_, at, side) in enumerate(slices):
        values = jnp.transpose(signed[:, index * width : (index + 1) * width])
        sent[at, side] = values.astype(jnp.bfloat16)


def module_kernel(
    table,
    early_held,
    late_held,
    master_held,
    momentum_held,
    new_master,
    new_momentum,
    first_out,
    second_out,
    totals,
    counts,
    early,
    late,
    master,
    momentum,
    arrived,
):
    paths = late.shape[0]
    modules, rows, _ = master.shape
    span = paths // CHUNKS
    pairs = []
    for chunk in range(CHUNKS):
        at = pl.ds(chunk * span, span)
        pairs.append((early_held.at[at], early.at[at]))
        pairs.append((late_held.at[at], late.at[at]))
    pairs += [(master_held, master), (momentum_held, momentum)]
    copies = [
        pltpu.make_async_copy(held, here, arrived.at[i]) for i, (held, here) in enumerate(pairs)
    ]
    for copy in copies:
        copy.start()
    totals[...] = jnp.zeros_like(totals)

    def clear(k, carry):
        counts[k] = 0
        return carry

    lax.fori_loop(0, modules, clear, 0)

    def visit(p, carry):
        module = table[p]
        counts[module] = counts[module] + 1
        signed = late[p].astype(jnp.float32)
        size = jnp.abs(signed)
        gradient = signed * lax.rsqrt(jnp.maximum(size, TINY))
        old = early[p, 0:rows].astype(jnp.float32)
        first = early[p, rows : 2 * rows].astype(jnp.float32)
        second = early[p, 2 * rows : 3 * rows].astype(jnp.float32)
        first = beta_first * first + (1.0 - beta_first) * gradient
        second = beta_second * second + (1.0 - beta_second) * size
        root = second * lax.rsqrt(second)
        new = old - inner_rate * (first / (root + epsilon) + decay_rate * old)
        for index, values in enumerate((new, first, second)):
            totals[index, module] += values.astype(jnp.bfloat16).astype(jnp.float32)
        return carry

    for chunk in range(CHUNKS):
        copies[2 * chunk].wait()
        copies[2 * chunk + 1].wait()
        lax.fori_loop(chunk * span, (chunk + 1) * span, visit, 0, unroll=8)
    for copy in copies[2 * CHUNKS :]:
        copy.wait()

    def finish(k, carry):
        count = counts[k]
        divisor = jnp.maximum(count, 1).astype(jnp.float32)
        old = master[k]
        delta = jnp.where(count > 0, old - totals[0, k] / divisor, jnp.zeros_like(old))
        moved = nesterov * momentum[k] + delta
        new_momentum[k] = moved
        new_master[k] = old - outer_rate * (delta + nesterov * moved)
        first_out[k] = (totals[1, k] / divisor).astype(jnp.bfloat16)
        second_out[k] = (totals[2, k] / divisor).astype(jnp.bfloat16)
        return carry

    lax.fori_loop(0, modules, finish, 0, unroll=4)


def whole(count):
    return [pl.BlockSpec(memory_space=pltpu.VMEM) for _ in range(count)]


def in_hbm(count):
    return [pl.BlockSpec(memory_space=pltpu.HBM) for _ in range(count)]


def per_device(
    token_pool,
    batch_ids,
    module_table,
    cotangent,
    path_weights,
    first_moment,
    second_moment,
    master_weights,
    outer_momentum,
):
    stations = lax.axis_size("y")
    groups = lax.axis_size("z") * lax.axis_size("x")
    pool, width = token_pool.shape
    features = path_weights.shape[1]
    rows = features // groups
    tokens = batch_ids.shape[1]
    path_axes = ("z", "x")

    fsdp_axes = ("y", "core")
    spot, core = lax.axis_index("y"), lax.axis_index("core")

    def swap(values):
        return lax.ppermute(values, "core", [(0, 1), (1, 0)])

    def hop(values, by):
        ways = [(2 * i, 2 * ((i + by) % stations)) for i in range(stations)]
        ways += [(2 * i + 1, 2 * ((i - by) % stations) + 1) for i in range(stations)]
        return lax.ppermute(values, fsdp_axes, ways)

    packed = pl.pallas_call(
        pack_kernel,
        out_shape=jax.ShapeDtypeStruct((groups, 3 * rows, width), jnp.bfloat16),
        in_specs=in_hbm(3),
        out_specs=pl.BlockSpec(memory_space=pltpu.HBM),
        scratch_shapes=[
            pltpu.VMEM((groups, 3 * rows, width), jnp.bfloat16),
            pltpu.SemaphoreType.DMA((CHUNKS, 3)),
            pltpu.SemaphoreType.DMA((CHUNKS,)),
        ],
        compiler_params=pltpu.CompilerParams(vmem_limit_bytes=56 * MIB),
        cost_estimate=pl.CostEstimate(flops=0, bytes_accessed=3 * MIB, transcendentals=0),
        name="pack",
    )(*[v[0].reshape(groups, rows, width) for v in (path_weights, first_moment, second_moment)])

    chip = jnp.stack([token_pool, swap(token_pool)])
    half = pool // 2
    held = {1: hop(chip, 1), 2: hop(chip, 2)}
    held[3] = hop(held[1], 2)
    held[4] = hop(lax.dynamic_slice_in_dim(held[2], core * half, half, axis=1), 2)
    near = jnp.concatenate([held[by].reshape(-1, width) for by in sorted(held)])
    far = swap(near)

    early = lax.all_to_all(packed, path_axes, 0, 0, tiled=True)

    onehot = (
        batch_ids[0][:, None] == lax.broadcasted_iota(jnp.int32, (tokens, pool), 1)
    ).astype(jnp.bfloat16)
    place = jnp.stack([spot, core]).astype(jnp.int32)

    sent = pl.pallas_call(
        gradient_kernel,
        out_shape=jax.ShapeDtypeStruct((stations, 2, width, width), jnp.bfloat16),
        in_specs=[pl.BlockSpec(memory_space=pltpu.SMEM)] + whole(6),
        out_specs=pl.BlockSpec(memory_space=pltpu.VMEM),
        compiler_params=pltpu.CompilerParams(vmem_limit_bytes=20 * MIB),
        cost_estimate=pl.CostEstimate(
            flops=2_000_000_000, bytes_accessed=5 * MIB, transcendentals=tokens * width
        ),
        name="path_gradient",
    )(place, chip, near, far, onehot, cotangent[0], path_weights[0].reshape(stations, 2, width, width))

    sent, early = lax.optimization_barrier((sent, early))
    late = lax.all_to_all(sent.reshape(groups, rows, width), path_axes, 0, 0, tiled=True)

    shape = master_weights.shape
    return pl.pallas_call(
        module_kernel,
        out_shape=(
            jax.ShapeDtypeStruct(shape, jnp.float32),
            jax.ShapeDtypeStruct(shape, jnp.float32),
            jax.ShapeDtypeStruct(shape, jnp.bfloat16),
            jax.ShapeDtypeStruct(shape, jnp.bfloat16),
        ),
        in_specs=[pl.BlockSpec(memory_space=pltpu.SMEM)] + in_hbm(4),
        out_specs=tuple(whole(4)),
        scratch_shapes=[
            pltpu.VMEM((3,) + shape, jnp.float32),
            pltpu.SMEM((shape[0],), jnp.int32),
            pltpu.VMEM((groups, 3 * rows, width), jnp.bfloat16),
            pltpu.VMEM((groups, rows, width), jnp.bfloat16),
            pltpu.VMEM(shape, jnp.float32),
            pltpu.VMEM(shape, jnp.float32),
            pltpu.SemaphoreType.DMA((2 * CHUNKS + 2,)),
        ],
        compiler_params=pltpu.CompilerParams(vmem_limit_bytes=56 * MIB),
        cost_estimate=pl.CostEstimate(
            flops=10_000_000, bytes_accessed=4 * MIB, transcendentals=4 * groups * rows * width
        ),
        name="module_update",
    )(module_table, early, late, master_weights, outer_momentum)


def solution(mesh):
    lengths = (8, 8, 8, 2)
    split = Mesh(mesh.devices.reshape(lengths), ("z", "x", "y", "core"))
    path = ("z", "x")
    fsdp = ("y", "core")
    in_specs = (
        P(None, fsdp),
        P(path, None),
        P(),
        P(path, None, fsdp),
        P(path, None, fsdp),
        P(path, None, fsdp),
        P(path, None, fsdp),
        P(None, path, fsdp),
        P(None, path, fsdp),
    )
    out_specs = (P(None, path, fsdp),) * 4
    return jax.shard_map(
        per_device, mesh=split, in_specs=in_specs, out_specs=out_specs, check_vma=False
    )
```
